256 devices in a mesh: seq: 32 (over z, y), head: 8 (over x, core).
Axes of the slice: x: 4, y: 4, z: 8, core: 2. Of those that a mesh axis runs over, the one named last changes fastest.
Arguments:
- query_rows: bfloat16 [65536, 4096], P(('seq', 'head')), may hold values from -6 to 6
- key_rows: bfloat16 [65536, 4096], P(('seq', 'head')), may hold values from -6 to 6
- value_rows: bfloat16 [65536, 4096], P(('seq', 'head')), may hold values from -6 to 6
- norm_gain: float32 [4096], P('head'), may hold values from 0.1 to 1.9
Outputs:
- mixed: bfloat16 [65536, 4096], P('seq', 'head')
The draws below stay inside these ranges and needn't reach their ends.
All inputs are finite; a program needn't handle non-finite values.
Results may differ from the reference program's by a relative error of at most 0.0027.
Values may be sent and summed in bfloat16 or wider, within the bound.
A program may use at most 128 MiB of HBM per device.

```python
import jax
import jax.numpy as jnp
from jax import lax

E = 128
H = 32
D = 4096
BLOCK = 512
L = 65536


def levels(key, dims, cuts, low, top_value):
    def one(dim, blocks):
        heights = jax.random.uniform(jax.random.fold_in(jax.random.fold_in(key, 6), dim), (blocks,), jnp.float32, low / len(cuts), top_value / len(cuts))
        return jnp.repeat(jnp.exp(heights), dims[dim] // blocks).reshape((-1,) + (1,) * (len(dims) - dim - 1))

    factor_of = one(*cuts[0])
    for cut in cuts[1:]:
        factor_of = factor_of * one(*cut)
    return factor_of


def centred(key, shape, deviation, reach, cuts=(), kind=jnp.bfloat16):
    drawn = deviation * jax.random.normal(key, shape, jnp.float32)
    if cuts:
        drawn = drawn * levels(key, shape, cuts, -0.22, 0.18)
    return jnp.clip(drawn, -reach, reach).astype(kind)


def setup_inputs(seed: int = 0) -> dict:
    key_of = jax.random.split(jax.random.key(seed), 5)
    query_rows = centred(key_of[0], (L, D), 1.0, 6.0, ((0, 256),))
    key_rows = centred(key_of[1], (L, D), 1.0, 6.0, ((0, 256),))
    value_rows = centred(key_of[2], (L, D), 1.0, 6.0, ((0, 256),))
    norm_gain = jnp.clip(1.0 + 0.18 * jax.random.normal(key_of[3], (D,), jnp.float32), 0.1, 1.9)
    return dict(query_rows=query_rows, key_rows=key_rows, value_rows=value_rows, norm_gain=norm_gain)


def reference(query_rows, key_rows, value_rows, norm_gain):
    total = query_rows.shape[0]
    blocks = total // BLOCK
    query_heads = query_rows.reshape(blocks, BLOCK, H, E)
    key_heads = key_rows.reshape(blocks, BLOCK, H, E)
    value_heads = value_rows.reshape(blocks, BLOCK, H, E)
    rowpos = lax.broadcasted_iota(jnp.int32, (BLOCK, BLOCK), 0)
    colpos = lax.broadcasted_iota(jnp.int32, (BLOCK, BLOCK), 1)
    causal = colpos <= rowpos
    highest = lax.Precision.HIGHEST

    def advance(running, pieces):
        query_blk, key_blk, value_blk = pieces
        query_f = query_blk.astype(jnp.float32)
        key_f = key_blk.astype(jnp.float32)
        value_f = value_blk.astype(jnp.float32)
        scores = jnp.einsum('bhe,che->hbc', query_f, key_f, precision=highest)
        scores = jnp.where(causal[None], scores, 0.0).astype(jnp.bfloat16)
        scores = lax.optimization_barrier(scores).astype(jnp.float32)
        within = jnp.einsum('hbc,che->bhe', scores, value_f, precision=highest)
        carried = jnp.einsum('bhe,hef->bhf', query_f, running, precision=highest)
        running = running + jnp.einsum('bhe,bhf->hef', key_f, value_f, precision=highest)
        return (running, carried + within)
    start_state = jnp.zeros((H, E, E), jnp.float32)
    _, attended = lax.scan(advance, start_state, (query_heads, key_heads, value_heads))
    attended = attended.reshape(total, H, E)
    scale_rms = jnp.sqrt(lax.optimization_barrier(jnp.mean(attended * attended, axis=-1, keepdims=True)) + 1e-06)
    normed = (attended / scale_rms).reshape(total, H * E) * norm_gain
    return normed.astype(jnp.bfloat16)
```

```python
import functools

import jax
import jax.numpy as jnp
from jax import lax
from jax.experimental import pallas as pl
from jax.experimental.pallas import tpu as pltpu
from jax.sharding import PartitionSpec as P

E = 128
TOKENS = 256
NX, NY, NZ, CORES = 4, 4, 8, 2
CHIPS = NX * NY
GROUP = NX * CORES
SETS = 2
PIECE = E // 2
STEPS = 4
SCALE = 1024.0
MESH = pl.DeviceIdType.MESH


def encode(state):
    scaled = state * SCALE
    return ((scaled * jnp.abs(scaled)) * (scaled * scaled)).astype(jnp.bfloat16)


def decode(code):
    wide = code.astype(jnp.float32)
    root = lax.rsqrt(lax.rsqrt(jnp.abs(wide))) * (1.0 / SCALE)
    return jnp.where(wide < 0.0, -root, root)


def kernel(q_hbm, k_hbm, v_hbm, gain_ref, out_hbm,
           q, k, v, own, sib, within, coded, landed, ahead, zcode, zland, pcode, pstate, result, gmine, gall,
           load_sem, sib_send, sib_recv, fwd_send, fwd_recv, z_send, z_recv, back_send, back_recv,
           pair_send, pair_recv, out_send, out_recv, gain_send, gain_recv):
    seq, me = lax.axis_index("seq"), lax.axis_index("head")
    z, y = lax.div(seq, NY), lax.rem(seq, NY)
    x, c = lax.div(me, CORES), lax.rem(me, CORES)
    n = y * NX + x

    def chip(a):
        return (z * NY + lax.div(a, NX), lax.rem(a, NX) * CORES + c)

    def depth(step):
        return (lax.rem(z + step, NZ) * NY + y, me)

    other = (seq, x * CORES + 1 - c)

    def turned(i):
        return lax.rem(n + 1 + i, CHIPS)

    def columns(h):
        return pl.ds(pl.multiple_of(h * E, E), E)

    def head_of(s, a):
        return 4 * lax.div(a, 2) + 2 * s + lax.rem(a, 2)

    half = pl.ds(pl.multiple_of(c * PIECE, PIECE), PIECE)

    loads = [
        pltpu.make_async_copy(src, dst, load_sem.at[i])
        for i, (src, dst) in enumerate(((k_hbm, k), (v_hbm, v), (q_hbm, q)))
    ]
    for load in loads:
        load.start()

    barrier = pltpu.get_barrier_semaphore()

    @pl.loop(1, CHIPS)
    def _(i):
        pl.semaphore_signal(barrier, inc=1, device_id=chip(lax.rem(n + i, CHIPS)), device_id_type=MESH)

    @pl.loop(1, NZ)
    def _(i):
        pl.semaphore_signal(barrier, inc=1, device_id=depth(i), device_id_type=MESH)

    @pl.loop(0, NX)
    def _(i):
        pl.semaphore_signal(
            barrier, inc=1, device_id=(seq, lax.rem(x + i, NX) * CORES + 1 - c), device_id_type=MESH
        )

    loads[0].wait()
    loads[1].wait()

    def sib_copy(s, g):
        part = pl.ds(g * STEPS, STEPS)
        return pltpu.make_async_remote_copy(
            own.at[s, part], sib.at[s, part], sib_send.at[s, g], sib_recv.at[s, g],
            device_id=other, device_id_type=MESH,
        )

    def outer(s, i):
        col = columns(head_of(s, turned(i)))
        own[s, i] = lax.dot_general(
            k[:, col], v[:, col], (((0,), (0,)), ((), ())), preferred_element_type=jnp.float32
        )

    @pl.loop(0, STEPS)
    def _(i):
        outer(0, i)

    pl.semaphore_wait(barrier, CHIPS - 1 + NZ - 1 + NX)
    sib_copy(0, 0).start()

    for s in range(SETS):
        @pl.loop(1 if s == 0 else 0, CHIPS // STEPS)
        def _(g):
            @pl.loop(0, STEPS)
            def _(u):
                outer(s, g * STEPS + u)
            sib_copy(s, g).start()

    def gain_copy(i):
        j = lax.rem(me + i, GROUP)
        return pltpu.make_async_remote_copy(
            gmine, gall.at[me], gain_send.at[i], gain_recv.at[me], device_id=(seq, j), device_id_type=MESH
        )

    def gain_landing(i):
        j = lax.rem(me + i, GROUP)
        return pltpu.make_async_remote_copy(
            gmine, gall.at[j], gain_send.at[i], gain_recv.at[j], device_id=(seq, j), device_id_type=MESH
        )

    def fwd_copy(s, i):
        return pltpu.make_async_remote_copy(
            coded.at[s, i], landed.at[s, n], fwd_send.at[s, i], fwd_recv.at[s, n],
            device_id=chip(turned(i)), device_id_type=MESH,
        )

    def fwd_landing(s, a):
        return pltpu.make_async_remote_copy(
            coded.at[s, 0], landed.at[s, a], fwd_send.at[s, 0], fwd_recv.at[s, a],
            device_id=chip(a), device_id_type=MESH,
        )

    def z_copy(s, i):
        return pltpu.make_async_remote_copy(
            zcode.at[s], zland.at[s, z], z_send.at[s, i], z_recv.at[s, z],
            device_id=depth(i), device_id_type=MESH,
        )

    def z_landing(s, i):
        origin = lax.rem(z + i, NZ)
        return pltpu.make_async_remote_copy(
            zcode.at[s], zland.at[s, origin], z_send.at[s, i], z_recv.at[s, origin],
            device_id=depth(i), device_id_type=MESH,
        )

    def back_copy(s, i):
        return pltpu.make_async_remote_copy(
            pcode.at[s, i], pstate.at[s, c, n], back_send.at[s, i], back_recv.at[s, n],
            device_id=chip(turned(i)), device_id_type=MESH,
        )

    def back_landing(s, a):
        return pltpu.make_async_remote_copy(
            pcode.at[s, 0], pstate.at[s, c, a], back_send.at[s, 0], back_recv.at[s, a],
            device_id=chip(a), device_id_type=MESH,
        )

    def pair_copy(s, which):
        return pltpu.make_async_remote_copy(
            pstate.at[s, which], pstate.at[s, which], pair_send.at[s], pair_recv.at[s],
            device_id=other, device_id_type=MESH,
        )

    def out_copy(s, t):
        return pltpu.make_async_remote_copy(
            result.at[s, t],
            out_hbm.at[pl.ds(pl.multiple_of(me * TOKENS, TOKENS), TOKENS), pl.ds(s * 2 * E, 2 * E)],
            out_send.at[s, t], out_recv.at[s, me],
            device_id=(seq, lax.rem(me + 1 + t, GROUP)), device_id_type=MESH,
        )

    def out_landing(s, t):
        j = lax.rem(me + 1 + t, GROUP)
        return pltpu.make_async_remote_copy(
            result.at[s, t],
            out_hbm.at[pl.ds(pl.multiple_of(j * TOKENS, TOKENS), TOKENS), pl.ds(s * 2 * E, 2 * E)],
            out_send.at[s, t], out_recv.at[s, j],
            device_id=(seq, j), device_id_type=MESH,
        )

    def out_local(s):
        return pltpu.make_async_copy(
            result.at[s, GROUP - 1],
            out_hbm.at[pl.ds(pl.multiple_of(me * TOKENS, TOKENS), TOKENS), pl.ds(s * 2 * E, 2 * E)],
            out_send.at[s, GROUP - 1],
        )

    for s in range(SETS):
        @pl.loop(0, CHIPS // STEPS)
        def _(g):
            sib_copy(s, g).wait_recv()

            @pl.loop(0, STEPS)
            def _(u):
                i = g * STEPS + u
                coded[s, i] = encode(own[s, i, half, :] + sib[s, i, half, :])

                @pl.when(i < CHIPS - 1)
                def _():
                    fwd_copy(s, i).start()

                @pl.when(i == CHIPS - 1)
                def _():
                    landed[s, n] = coded[s, i]

    gmine[...] = jnp.broadcast_to(gain_ref[...], gmine.shape)
    gall[me] = jnp.broadcast_to(gain_ref[...], gmine.shape)

    @pl.loop(1, GROUP)
    def _(i):
        gain_copy(i).start()

    loads[2].wait()
    causal = lax.broadcasted_iota(jnp.int32, (TOKENS, TOKENS), 1) <= lax.broadcasted_iota(
        jnp.int32, (TOKENS, TOKENS), 0
    )

    def inside(h):
        col = columns(h)
        scores = lax.dot_general(
            q[:, col], k[:, col], (((1,), (1,)), ((), ())), preferred_element_type=jnp.float32
        )
        weights = jnp.where(causal, scores, 0.0).astype(jnp.bfloat16)
        within[h] = jnp.dot(weights, v[:, col], preferred_element_type=jnp.float32)

    def inside_part(first, last):
        @pl.loop(first, last)
        def _(h):
            inside(h)

    def gather_plane(s):
        @pl.loop(1, CHIPS)
        def _(i):
            fwd_landing(s, lax.rem(n + CHIPS - i, CHIPS)).wait_recv()

        def add(a, total):
            ahead[s, a] = total
            return total + decode(landed[s, a])

        total = lax.fori_loop(0, CHIPS, add, jnp.zeros((PIECE, E), jnp.float32))
        zcode[s] = encode(total)

        @pl.loop(1, NZ)
        def _(i):
            z_copy(s, i).start()

    def give_back(s):
        def add(i, base):
            origin = lax.rem(z + i, NZ)
            z_landing(s, i).wait_recv()
            return base + jnp.where(origin < z, decode(zland[s, origin]), 0.0)

        base = lax.fori_loop(1, NZ, add, jnp.zeros((PIECE, E), jnp.float32))

        @pl.loop(0, CHIPS)
        def _(i):
            pcode[s, i] = encode(base + ahead[s, turned(i)])

            @pl.when(i < CHIPS - 1)
            def _():
                back_copy(s, i).start()

            @pl.when(i == CHIPS - 1)
            def _():
                pstate[s, c, n] = pcode[s, i]

    def share(s):
        @pl.loop(1, CHIPS)
        def _(i):
            back_landing(s, lax.rem(n + CHIPS - i, CHIPS)).wait_recv()
        pair_copy(s, c).start()

    def finish(s):
        pair_copy(s, 1 - c).wait_recv()

        @pl.loop(0, GROUP)
        def _(t):
            j = lax.rem(me + 1 + t, GROUP)
            for u in range(2):
                a = 2 * j + u
                h = 4 * j + 2 * s + u
                col = columns(h)
                before = jnp.concatenate([decode(pstate[s, 0, a]), decode(pstate[s, 1, a])], axis=0)
                beside = sib[s, lax.rem(a - n - 1 + CHIPS, CHIPS)]
                before = before + jnp.where(c == 1, beside, 0.0)
                high = before.astype(jnp.bfloat16)
                low = (before - high.astype(jnp.float32)).astype(jnp.bfloat16)
                queries = q[:, col]
                attended = (
                    within[h]
                    + jnp.dot(queries, high, preferred_element_type=jnp.float32)
                    + jnp.dot(queries, low, preferred_element_type=jnp.float32)
                )
                mean = jnp.mean(attended * attended, axis=-1, keepdims=True)
                gain = gall[j, 0:1, (2 * s + u) * E:(2 * s + u + 1) * E]
                normed = attended * lax.rsqrt(mean + 1e-06) * gain
                result[s, t, :, u * E:(u + 1) * E] = normed.astype(jnp.bfloat16)

            @pl.when(t < GROUP - 1)
            def _():
                out_copy(s, t).start()

            @pl.when(t == GROUP - 1)
            def _():
                out_local(s).start()

    inside_part(0, 8)
    gather_plane(0)
    inside_part(8, 16)
    gather_plane(1)
    inside_part(16, 32)
    give_back(0)
    give_back(1)

    @pl.loop(1, GROUP)
    def _(i):
        gain_landing(i).wait_recv()

    share(0)
    finish(0)
    share(1)
    finish(1)

    for s in range(SETS):
        out_local(s).wait()

        @pl.loop(0, GROUP - 1)
        def _(t):
            out_landing(s, t).wait_recv()

        @pl.loop(0, GROUP - 1)
        def _(t):
            out_copy(s, t).wait_send()

        @pl.loop(0, CHIPS // STEPS)
        def _(g):
            sib_copy(s, g).wait_send()

        @pl.loop(0, CHIPS - 1)
        def _(i):
            fwd_copy(s, i).wait_send()
            back_copy(s, i).wait_send()

        @pl.loop(1, NZ)
        def _(i):
            z_copy(s, i).wait_send()

        pair_copy(s, c).wait_send()

    @pl.loop(1, GROUP)
    def _(i):
        gain_copy(i).wait_send()


def shards(query_rows, key_rows, value_rows, norm_gain):
    tokens, width = query_rows.shape
    heads = width // E
    dma = pltpu.SemaphoreType.DMA
    return pl.pallas_call(
        kernel,
        out_shape=jax.ShapeDtypeStruct((tokens * GROUP, width // GROUP), jnp.bfloat16),
        in_specs=[pl.BlockSpec(memory_space=pl.ANY)] * 3 + [pl.BlockSpec(memory_space=pltpu.VMEM)],
        out_specs=pl.BlockSpec(memory_space=pl.ANY),
        scratch_shapes=[
            pltpu.VMEM((tokens, width), jnp.bfloat16),
            pltpu.VMEM((tokens, width), jnp.bfloat16),
            pltpu.VMEM((tokens, width), jnp.bfloat16),
            pltpu.VMEM((SETS, CHIPS, E, E), jnp.float32),
            pltpu.VMEM((SETS, CHIPS, E, E), jnp.float32),
            pltpu.VMEM((heads, tokens, E), jnp.float32),
            pltpu.VMEM((SETS, CHIPS, PIECE, E), jnp.bfloat16),
            pltpu.VMEM((SETS, CHIPS, PIECE, E), jnp.bfloat16),
            pltpu.VMEM((SETS, CHIPS, PIECE, E), jnp.float32),
            pltpu.VMEM((SETS, PIECE, E), jnp.bfloat16),
            pltpu.VMEM((SETS, NZ, PIECE, E), jnp.bfloat16),
            pltpu.VMEM((SETS, CHIPS, PIECE, E), jnp.bfloat16),
            pltpu.VMEM((SETS, CORES, CHIPS, PIECE, E), jnp.bfloat16),
            pltpu.VMEM((SETS, GROUP, tokens, 2 * E), jnp.bfloat16),
            pltpu.VMEM((8, 4 * E), jnp.float32),
            pltpu.VMEM((GROUP, 8, 4 * E), jnp.float32),
            dma((3,)),
            dma((SETS, CHIPS // STEPS)), dma((SETS, CHIPS // STEPS)),
            dma((SETS, CHIPS)), dma((SETS, CHIPS)),
            dma((SETS, NZ)), dma((SETS, NZ)),
            dma((SETS, CHIPS)), dma((SETS, CHIPS)),
            dma((SETS,)), dma((SETS,)),
            dma((SETS, GROUP)), dma((SETS, GROUP)),
            dma((GROUP,)), dma((GROUP,)),
        ],
        compiler_params=pltpu.CompilerParams(
            collective_id=0, has_side_effects=True, vmem_limit_bytes=48 * 1024 * 1024
        ),
    )(query_rows, key_rows, value_rows, norm_gain.reshape(1, 4 * E))


def solution(mesh):
    placed = (
        P(("seq", "head"), None),
        P(("seq", "head"), None),
        P(("seq", "head"), None),
        P("head"),
    )
    return jax.shard_map(
        shards, mesh=mesh, in_specs=placed, out_specs=P("seq", "head"), check_vma=False
    )
```

```python
import jax
import jax.numpy as jnp
from jax import lax
from jax.experimental import pallas as pl
from jax.experimental.pallas import tpu as pltpu
from jax.sharding import PartitionSpec as P

E = 128
TOKENS = 256
HEADS = 32
NX, NY, NZ, CORES = 4, 4, 8, 2
CHIPS = NX * NY
GROUP = NX * CORES
SETS = 4
PER_SET = HEADS // SETS
SUBS = CHIPS // PER_SET
PER_DEST = PER_SET // GROUP
PIECE = E // (SUBS * CORES)
CHUNKS = 4
SCALE = 1024.0
MESH = pl.DeviceIdType.MESH


def encode(state):
    scaled = state * SCALE
    return ((scaled * jnp.abs(scaled)) * (scaled * scaled)).astype(jnp.bfloat16)


def decode(code):
    wide = code.astype(jnp.float32)
    root = lax.rsqrt(lax.rsqrt(jnp.abs(wide))) * (1.0 / SCALE)
    return jnp.where(wide < 0.0, -root, root)


def kernel(q_hbm, k_hbm, v_hbm, gain_hbm, out_hbm,
           q, k, v, own, sib, within, coded, landed, ahead, zcode, zland, pcode, pstate, result, grow, gmine, gall,
           load_sem, own_send, near_recv, rest_recv, fwd_send, fwd_recv, z_send, z_recv, back_send, back_recv,
           pair_send, pair_recv, out_send, out_recv, out_keep, gain_send, gain_recv, z_ready):
    seq, me = lax.axis_index("seq"), lax.axis_index("head")
    z, y = lax.div(seq, NY), lax.rem(seq, NY)
    x, c = lax.div(me, CORES), lax.rem(me, CORES)
    n = y * NX + x
    other = (seq, x * CORES + 1 - c)

    def chip(a):
        return (z * NY + lax.div(a, NX), lax.rem(a, NX) * CORES + c)

    def depth(other_z):
        return (other_z * NY + y, me)

    def turned(i):
        return lax.rem(n + 1 + i, CHIPS)

    def columns(h):
        if isinstance(h, int):
            return pl.ds(h * E, E)
        return pl.ds(pl.multiple_of(h * E, E), E)

    wide = HEADS * E // CHUNKS
    k_loads = [
        pltpu.make_async_copy(k_hbm.at[:, pl.ds(i * wide, wide)], k.at[:, pl.ds(i * wide, wide)], load_sem.at[2 * i])
        for i in range(CHUNKS)
    ]
    v_loads = [
        pltpu.make_async_copy(v_hbm.at[:, pl.ds(i * wide, wide)], v.at[:, pl.ds(i * wide, wide)], load_sem.at[2 * i + 1])
        for i in range(CHUNKS)
    ]
    q_load = pltpu.make_async_copy(q_hbm, q, load_sem.at[2 * CHUNKS])
    gain_load = pltpu.make_async_copy(gain_hbm, grow, load_sem.at[2 * CHUNKS + 1])
    for i in range(CHUNKS):
        k_loads[i].start()
        v_loads[i].start()
    q_load.start()
    gain_load.start()

    barrier = pltpu.get_barrier_semaphore()

    @pl.loop(1, CHIPS)
    def _(i):
        pl.semaphore_signal(barrier, inc=1, device_id=chip(lax.rem(n + i, CHIPS)), device_id_type=MESH)

    @pl.loop(0, NX)
    def _(i):
        pl.semaphore_signal(
            barrier, inc=1, device_id=(seq, lax.rem(x + i, NX) * CORES + 1 - c), device_id_type=MESH
        )

    @pl.loop(z + 1, NZ)
    def _(i):
        pl.semaphore_signal(barrier, inc=1, device_id=depth(i), device_id_type=MESH)

    for i in range(CHUNKS):
        k_loads[i].wait()
        v_loads[i].wait()
        for h in range(i * HEADS // CHUNKS, (i + 1) * HEADS // CHUNKS):
            state = lax.dot_general(
                k[:, columns(h)], v[:, columns(h)], (((0,), (0,)), ((), ())), preferred_element_type=jnp.float32
            )
            dest, place = h // 4, h % 4
            s, a = place // PER_DEST, dest * PER_DEST + place % PER_DEST
            for sub in range(SUBS):
                for core in range(CORES):
                    row = (sub * CORES + core) * PIECE
                    own[s, core, a * SUBS + sub] = state[row:row + PIECE]

    pl.semaphore_wait(barrier, CHIPS - 1 + NX + z)

    @pl.loop(0, z)
    def _(i):
        pl.semaphore_signal(z_ready, inc=1, device_id=depth(i), device_id_type=MESH)

    def near_copy(s, core):
        return pltpu.make_async_remote_copy(
            own.at[s, core], sib.at[s, core], own_send, near_recv.at[s], device_id=other, device_id_type=MESH
        )

    def rest_copy(part, core):
        return pltpu.make_async_remote_copy(
            own.at[part, core], sib.at[part, core], own_send, rest_recv, device_id=other, device_id_type=MESH
        )

    for s in range(SETS):
        near_copy(s, 1 - c).start()
    for s in range(SETS):
        rest_copy(s, c).start()

    def gain_copy(i, src, dst):
        return pltpu.make_async_remote_copy(
            src, dst, gain_send, gain_recv, device_id=(seq, lax.rem(me + i, GROUP)), device_id_type=MESH
        )

    def fwd_copy(s, a, src, dst):
        return pltpu.make_async_remote_copy(
            src, dst, fwd_send, fwd_recv.at[s], device_id=chip(a), device_id_type=MESH
        )

    def z_copy(s, i, src, dst):
        return pltpu.make_async_remote_copy(
            src, dst, z_send, z_recv.at[s], device_id=depth(i), device_id_type=MESH
        )

    def back_copy(s, a, src, dst):
        return pltpu.make_async_remote_copy(
            src, dst, back_send, back_recv.at[s], device_id=chip(a), device_id_type=MESH
        )

    def pair_copy(s, which):
        return pltpu.make_async_remote_copy(
            pstate.at[s, which], pstate.at[s, which], pair_send, pair_recv.at[s],
            device_id=other, device_id_type=MESH,
        )

    def out_place(s, j):
        return out_hbm.at[
            pl.ds(pl.multiple_of(j * TOKENS, TOKENS), TOKENS), pl.ds(s * PER_DEST * E, PER_DEST * E)
        ]

    def out_copy(t, src, dst):
        return pltpu.make_async_remote_copy(
            src, dst, out_send, out_recv, device_id=(seq, lax.rem(me + 1 + t, GROUP)), device_id_type=MESH
        )

    def out_local(part, place):
        return pltpu.make_async_copy(result.at[part, GROUP - 1], place, out_keep)

    most, peers = pl.ds(0, CHIPS - 1), pl.ds(0, GROUP - 1)

    for s in range(SETS):
        near_copy(s, c).wait_recv()

        @pl.loop(0, CHIPS)
        def _(i):
            a = turned(i)
            coded[s, i] = encode(own[s, c, a] + sib[s, c, a])

        @pl.loop(0, CHIPS - 1)
        def _(i):
            fwd_copy(s, turned(i), coded.at[s, i], landed.at[s, n]).start()

        landed[s, n] = coded[s, CHIPS - 1]

    gain_load.wait()
    gmine[...] = jnp.broadcast_to(grow[...], gmine.shape)
    gall[me] = jnp.broadcast_to(grow[...], gmine.shape)

    @pl.loop(1, GROUP)
    def _(i):
        gain_copy(i, gmine, gall.at[me]).start()

    q_load.wait()

    def inside_part(first, last):
        causal = lax.broadcasted_iota(jnp.int32, (TOKENS, TOKENS), 1) <= lax.broadcasted_iota(
            jnp.int32, (TOKENS, TOKENS), 0
        )

        @pl.loop(first // 8, last // 8)
        def _(group):
            for u in range(8):
                h = group * 8 + u
                col = columns(h)
                scores = lax.dot_general(
                    q[:, col], k[:, col], (((1,), (1,)), ((), ())), preferred_element_type=jnp.float32
                )
                weights = jnp.where(causal, scores, 0.0).astype(jnp.bfloat16)
                within[h] = jnp.dot(weights, v[:, col], preferred_element_type=jnp.float32)

    def gather_plane(s):
        fwd_copy(s, n, coded.at[s, most], landed.at[s, most]).wait_recv()
        total = jnp.zeros((PIECE, E), jnp.float32)
        for a in range(CHIPS):
            ahead[s, a] = total
            total = total + decode(landed[s, a])
        zcode[s] = encode(total)
        if s == 0:
            @pl.when(z < NZ - 1)
            def _():
                pl.semaphore_wait(z_ready, NZ - 1 - z)

        @pl.loop(z + 1, NZ)
        def _(i):
            z_copy(s, i, zcode.at[s], zland.at[s, z]).start()

    def give_back(s):
        for count in range(1, NZ):
            @pl.when(z == count)
            def _():
                z_copy(s, z, zland.at[s, pl.ds(0, count)], zland.at[s, pl.ds(0, count)]).wait_recv()

        def add(i, base):
            return base + decode(zland[s, i])

        base = lax.fori_loop(0, z, add, jnp.zeros((PIECE, E), jnp.float32))
        for i in range(CHIPS):
            pcode[s, i] = encode(base + ahead[s, turned(i)])

        @pl.loop(0, CHIPS - 1)
        def _(i):
            back_copy(s, turned(i), pcode.at[s, i], pstate.at[s, c, n]).start()

        pstate[s, c, n] = pcode[s, CHIPS - 1]

    def share(s):
        back_copy(s, n, pcode.at[s, most], pstate.at[s, c, most]).wait_recv()
        pair_copy(s, c).start()

    def finish(s):
        pair_copy(s, 1 - c).wait_recv()
        if s == 0:
            rest_copy(pl.ds(0, SETS), 1 - c).wait_recv()
        for t in range(GROUP):
            j = lax.rem(me + 1 + t, GROUP)
            for u in range(PER_DEST):
                a = j * PER_DEST + u
                place = s * PER_DEST + u
                h = 4 * j + place
                pieces = [(core, a * SUBS + sub) for sub in range(SUBS) for core in range(CORES)]
                before = jnp.concatenate([decode(pstate[s, core, p]) for core, p in pieces], axis=0)
                beside = jnp.concatenate([sib[s, core, p] for core, p in pieces], axis=0)
                before = before + jnp.where(c == 1, beside, 0.0)
                high = before.astype(jnp.bfloat16)
                low = (before - high.astype(jnp.float32)).astype(jnp.bfloat16)
                queries = q[:, columns(h)]
                attended = (
                    within[h]
                    + jnp.dot(queries, high, preferred_element_type=jnp.float32)
                    + jnp.dot(queries, low, preferred_element_type=jnp.float32)
                )
                mean = jnp.mean(attended * attended, axis=-1, keepdims=True)
                gain = gall[j, 0:1, place * E:(place + 1) * E]
                normed = attended * lax.rsqrt(mean + 1e-06) * gain
                result[s, t, :, u * E:(u + 1) * E] = normed.astype(jnp.bfloat16)

        @pl.loop(0, GROUP - 1)
        def _(t):
            out_copy(t, result.at[s, t], out_place(s, me)).start()

        out_local(s, out_place(s, me)).start()

    inside_part(0, 16)
    gather_plane(0)
    inside_part(16, 24)
    gather_plane(1)
    inside_part(24, 32)
    gather_plane(2)
    give_back(0)
    gather_plane(3)
    give_back(1)
    give_back(2)
    give_back(3)
    gain_copy(0, gall.at[peers], gall.at[peers]).wait_recv()
    share(0)
    share(1)
    finish(0)
    share(2)
    finish(1)
    share(3)
    finish(2)
    finish(3)

    rows = pl.ds(0, (GROUP - 1) * TOKENS)
    out_copy(0, out_hbm.at[rows], out_hbm.at[rows]).wait_recv()
    pltpu.make_async_copy(out_hbm.at[pl.ds(0, TOKENS)], out_hbm.at[pl.ds(0, TOKENS)], out_keep).wait()
    out_copy(0, result.at[:, peers], result.at[:, peers]).wait_send()
    pltpu.make_async_remote_copy(own, own, own_send, rest_recv, device_id=other, device_id_type=MESH).wait_send()
    fwd_copy(0, n, coded.at[:, most], coded.at[:, most]).wait_send()
    back_copy(0, n, pcode.at[:, most], pcode.at[:, most]).wait_send()
    for count in range(1, NZ):
        @pl.when(z == NZ - 1 - count)
        def _():
            z_copy(0, z, zland.at[:, pl.ds(0, count)], zland.at[:, pl.ds(0, count)]).wait_send()
    pltpu.make_async_remote_copy(
        pstate.at[:, 0], pstate.at[:, 0], pair_send, pair_recv.at[0], device_id=other, device_id_type=MESH
    ).wait_send()
    gain_copy(0, gall.at[peers], gall.at[peers]).wait_send()


def shards(query_rows, key_rows, value_rows, norm_gain):
    tokens, width = query_rows.shape
    dma = pltpu.SemaphoreType.DMA
    f32, bf16 = jnp.float32, jnp.bfloat16
    held = [pltpu.with_memory_space_constraint(rows, pltpu.HBM) for rows in (query_rows, key_rows, value_rows, norm_gain.reshape(1, 4 * E))]
    return pl.pallas_call(
        kernel,
        out_shape=jax.ShapeDtypeStruct((tokens * GROUP, width // GROUP), bf16),
        in_specs=[pl.BlockSpec(memory_space=pl.ANY)] * 4,
        out_specs=pl.BlockSpec(memory_space=pl.ANY),
        scratch_shapes=[
            pltpu.VMEM((tokens, width), bf16),
            pltpu.VMEM((tokens, width), bf16),
            pltpu.VMEM((tokens, width), bf16),
            pltpu.VMEM((SETS, CORES, CHIPS, PIECE, E), f32),
            pltpu.VMEM((SETS, CORES, CHIPS, PIECE, E), f32),
            pltpu.VMEM((HEADS, tokens, E), f32),
            pltpu.VMEM((SETS, CHIPS, PIECE, E), bf16),
            pltpu.VMEM((SETS, CHIPS, PIECE, E), bf16),
            pltpu.VMEM((SETS, CHIPS, PIECE, E), f32),
            pltpu.VMEM((SETS, PIECE, E), bf16),
            pltpu.VMEM((SETS, NZ, PIECE, E), bf16),
            pltpu.VMEM((SETS, CHIPS, PIECE, E), bf16),
            pltpu.VMEM((SETS, CORES, CHIPS, PIECE, E), bf16),
            pltpu.VMEM((SETS, GROUP, tokens, PER_DEST * E), bf16),
            pltpu.VMEM((1, 4 * E), f32),
            pltpu.VMEM((8, 4 * E), f32),
            pltpu.VMEM((GROUP, 8, 4 * E), f32),
            dma((2 * CHUNKS + 2,)),
            dma, dma((SETS,)), dma,
            dma, dma((SETS,)), dma, dma((SETS,)), dma, dma((SETS,)),
            dma, dma((SETS,)),
            dma, dma, dma, dma, dma,
            pltpu.SemaphoreType.REGULAR,
        ],
        compiler_params=pltpu.CompilerParams(
            collective_id=0, has_side_effects=True, vmem_limit_bytes=48 * 1024 * 1024
        ),
    )(*held)


def solution(mesh):
    placed = (
        P(("seq", "head"), None),
        P(("seq", "head"), None),
        P(("seq", "head"), None),
        P("head"),
    )
    return jax.shard_map(
        shards, mesh=mesh, in_specs=placed, out_specs=P("seq", "head"), check_vma=False
    )
```

```python
import jax
import jax.numpy as jnp
from jax import lax
from jax.experimental import pallas as pl
from jax.experimental.pallas import tpu as pltpu
from jax.sharding import PartitionSpec as P

E = 128
TOKENS = 256
HEADS = 32
NX, NY, NZ, CORES = 4, 4, 8, 2
CHIPS = NX * NY
GROUP = NX * CORES
PER_DEVICE = HEADS // GROUP
EVEN, ODD, EVERY = tuple(range(0, GROUP, 2)), tuple(range(1, GROUP, 2)), tuple(range(GROUP))
SETS = ((0, EVEN), (0, ODD), (1, EVERY), (2, EVERY), (3, EVERY))
SIZES = [len(devices) for _, devices in SETS]
SUBS = [CHIPS // size for size in SIZES]
PIECES = [E * size // HEADS for size in SIZES]
ROWS = [slice(sum(PIECES[:s]), sum(PIECES[:s + 1])) for s in range(len(SETS))]
SCALE = 1024.0
MESH = pl.DeviceIdType.MESH


def encode(state):
    scaled = state * SCALE
    return ((scaled * jnp.abs(scaled)) * (scaled * scaled)).astype(jnp.bfloat16)


def decode(code):
    wide = code.astype(jnp.float32)
    root = lax.rsqrt(lax.rsqrt(jnp.abs(wide))) * (1.0 / SCALE)
    return jnp.where(wide < 0.0, -root, root)


def kernel(q_hbm, k_hbm, v_hbm, gain_hbm, out_hbm,
           q, k, v, own, sib, within, coded, landed, ahead, zcode, zland, pcode, pstate, result, grow, gmine, gall,
           load_sem, own_send, near_recv, rest_recv, fwd_send, fwd_recv, z_send, z_recv, back_send, back_recv,
           pair_send, pair_recv, out_send, out_recv, out_keep, gain_send, gain_recv, z_ready):
    seq, me = lax.axis_index("seq"), lax.axis_index("head")
    z, y = lax.div(seq, NY), lax.rem(seq, NY)
    x, c = lax.div(me, CORES), lax.rem(me, CORES)
    n = y * NX + x
    other = (seq, x * CORES + 1 - c)

    def chip(a):
        return (z * NY + lax.div(a, NX), lax.rem(a, NX) * CORES + c)

    def depth(other_z):
        return (other_z * NY + y, me)

    def turned(i):
        return lax.rem(n + 1 + i, CHIPS)

    def columns(h):
        if isinstance(h, int):
            return pl.ds(h * E, E)
        return pl.ds(pl.multiple_of(h * E, E), E)

    def loads(first, width, devices, sems):
        for j in devices:
            part = pl.ds(j * PER_DEVICE * E + first * E, width * E)
            for source, target, sem in ((k_hbm, k, sems[0]), (v_hbm, v, sems[1])):
                pltpu.make_async_copy(source.at[:, part], target.at[:, part], load_sem.at[sem]).start()

    def loaded(width, devices, sems):
        part = pl.ds(0, width * len(devices) * E)
        for source, target, sem in ((k_hbm, k, sems[0]), (v_hbm, v, sems[1])):
            pltpu.make_async_copy(source.at[:, part], target.at[:, part], load_sem.at[sem]).wait()

    q_load = pltpu.make_async_copy(q_hbm, q, load_sem.at[6])
    gain_load = pltpu.make_async_copy(gain_hbm, grow, load_sem.at[7])
    loads(0, 1, EVEN, (0, 1))
    loads(0, 4, ODD, (2, 3))
    loads(1, 3, EVEN, (4, 5))
    zland[...] = jnp.zeros_like(zland)

    barrier = pltpu.get_barrier_semaphore()

    @pl.loop(1, CHIPS)
    def _(i):
        pl.semaphore_signal(barrier, inc=1, device_id=chip(lax.rem(n + i, CHIPS)), device_id_type=MESH)

    @pl.loop(0, NX)
    def _(i):
        pl.semaphore_signal(
            barrier, inc=1, device_id=(seq, lax.rem(x + i, NX) * CORES + 1 - c), device_id_type=MESH
        )

    @pl.loop(z + 1, NZ)
    def _(i):
        pl.semaphore_signal(barrier, inc=1, device_id=depth(i), device_id_type=MESH)

    q_load.start()
    gain_load.start()

    def outer(s, a):
        place, devices = SETS[s]
        col = columns(devices[a] * PER_DEVICE + place)
        state = lax.dot_general(k[:, col], v[:, col], (((0,), (0,)), ((), ())), preferred_element_type=jnp.float32)
        for sub in range(SUBS[s]):
            for core in range(CORES):
                row = (sub * CORES + core) * PIECES[s]
                own[core, a * SUBS[s] + sub, ROWS[s]] = state[row:row + PIECES[s]]

    def own_copy(s, core, sem):
        part = (core, slice(None), ROWS[s])
        return pltpu.make_async_remote_copy(
            own.at[part], sib.at[part], own_send, sem, device_id=other, device_id_type=MESH
        )

    def gain_copy(i, src, dst):
        return pltpu.make_async_remote_copy(
            src, dst, gain_send, gain_recv, device_id=(seq, lax.rem(me + i, GROUP)), device_id_type=MESH
        )

    def fwd_copy(s, a, src, dst):
        return pltpu.make_async_remote_copy(
            src, dst, fwd_send, fwd_recv.at[s], device_id=chip(a), device_id_type=MESH
        )

    def z_copy(s, i, src, dst):
        return pltpu.make_async_remote_copy(
            src, dst, z_send, z_recv.at[s], device_id=depth(i), device_id_type=MESH
        )

    def back_copy(s, a, src, dst):
        return pltpu.make_async_remote_copy(
            src, dst, back_send, back_recv.at[s], device_id=chip(a), device_id_type=MESH
        )

    def pair_copy(s, which):
        part = (which, slice(None), ROWS[s])
        return pltpu.make_async_remote_copy(
            pstate.at[part], pstate.at[part], pair_send, pair_recv.at[s], device_id=other, device_id_type=MESH
        )

    def out_place(place, j):
        return out_hbm.at[pl.ds(pl.multiple_of(j * TOKENS, TOKENS), TOKENS), pl.ds(place * E, E)]

    def out_copy(j, src, dst):
        return pltpu.make_async_remote_copy(src, dst, out_send, out_recv, device_id=(seq, j), device_id_type=MESH)

    most, peers = pl.ds(0, CHIPS - 1), pl.ds(0, GROUP - 1)

    def outers(s):
        for a in range(SIZES[s]):
            outer(s, a)

    def send_near(s):
        own_copy(s, 1 - c, near_recv.at[s]).start()

    def forward(s):
        own_copy(s, c, near_recv.at[s]).wait_recv()
        rows = ROWS[s]
        for i in range(CHIPS):
            a = turned(i)
            coded[i, rows] = encode(own[c, a, rows] + sib[c, a, rows])

        @pl.loop(0, CHIPS - 1)
        def _(i):
            fwd_copy(s, turned(i), coded.at[i, rows], landed.at[n, rows]).start()

        landed[n, rows] = coded[CHIPS - 1, rows]

    def share_gain():
        gain_load.wait()
        gmine[...] = jnp.broadcast_to(grow[...], gmine.shape)
        gall[me] = jnp.broadcast_to(grow[...], gmine.shape)

        @pl.loop(1, GROUP)
        def _(i):
            gain_copy(i, gmine, gall.at[me]).start()

    def inside_part(first, last):
        causal = lax.broadcasted_iota(jnp.int32, (TOKENS, TOKENS), 1) <= lax.broadcasted_iota(
            jnp.int32, (TOKENS, TOKENS), 0
        )

        @pl.loop(first // 8, last // 8)
        def _(group):
            for u in range(8):
                h = group * 8 + u
                col = columns(h)
                scores = lax.dot_general(
                    q[:, col], k[:, col], (((1,), (1,)), ((), ())), preferred_element_type=jnp.float32
                )
                weights = jnp.where(causal, scores, 0.0).astype(jnp.bfloat16)
                within[h] = jnp.dot(weights, v[:, col], preferred_element_type=jnp.float32)

    def gather_plane(s):
        rows = ROWS[s]
        fwd_copy(s, n, coded.at[most, rows], landed.at[most, rows]).wait_recv()
        total = jnp.zeros((PIECES[s], E), jnp.float32)
        for a in range(CHIPS):
            ahead[a, rows] = total
            total = total + decode(landed[a, rows])
        zcode[rows] = encode(total)
        if s == 0:
            @pl.when(z < NZ - 1)
            def _():
                pl.semaphore_wait(z_ready, NZ - 1 - z)

        @pl.loop(z + 1, NZ)
        def _(i):
            z_copy(s, i, zcode.at[rows], zland.at[z, rows]).start()

    def give_back(s):
        rows = ROWS[s]
        for count in range(1, NZ):
            @pl.when(z == count)
            def _():
                earlier = zland.at[pl.ds(0, count), rows]
                z_copy(s, z, earlier, earlier).wait_recv()

        base = decode(zland[0, rows])
        for i in range(1, NZ - 1):
            base = base + decode(zland[i, rows])
        for i in range(CHIPS):
            pcode[i, rows] = encode(base + ahead[turned(i), rows])

        @pl.loop(0, CHIPS - 1)
        def _(i):
            back_copy(s, turned(i), pcode.at[i, rows], pstate.at[c, n, rows]).start()

        pstate[c, n, rows] = pcode[CHIPS - 1, rows]

    def share(s):
        rows = ROWS[s]
        back_copy(s, n, pcode.at[most, rows], pstate.at[c, most, rows]).wait_recv()
        pair_copy(s, c).start()

    def finish(s):
        pair_copy(s, 1 - c).wait_recv()
        rows = ROWS[s]
        place, devices = SETS[s]
        if s == 0:
            everything = sib.at[1 - c]
            pltpu.make_async_remote_copy(
                everything, everything, own_send, rest_recv, device_id=other, device_id_type=MESH
            ).wait_recv()
        for t in range(SIZES[s]):
            a = lax.rem(x * SIZES[s] // NX + 1 + t, SIZES[s])
            j = a * (GROUP // SIZES[s]) + devices[0]
            h = j * PER_DEVICE + place
            pieces = [(core, a * SUBS[s] + sub) for sub in range(SUBS[s]) for core in range(CORES)]
            before = jnp.concatenate([decode(pstate[core, p, rows]) for core, p in pieces], axis=0)
            beside = jnp.concatenate([sib[core, p, rows] for core, p in pieces], axis=0)
            before = before + jnp.where(c == 1, beside, 0.0)
            high = before.astype(jnp.bfloat16)
            low = (before - high.astype(jnp.float32)).astype(jnp.bfloat16)
            queries = q[:, columns(h)]
            attended = (
                within[h]
                + jnp.dot(queries, high, preferred_element_type=jnp.float32)
                + jnp.dot(queries, low, preferred_element_type=jnp.float32)
            )
            mean = jnp.mean(attended * attended, axis=-1, keepdims=True)
            gain = gall[j, 0:1, place * E:(place + 1) * E]
            normed = attended * lax.rsqrt(mean + 1e-06) * gain
            result[j, :, place * E:(place + 1) * E] = normed.astype(jnp.bfloat16)

        @pl.loop(0, SIZES[s])
        def _(t):
            a = lax.rem(x * SIZES[s] // NX + 1 + t, SIZES[s])
            j = a * (GROUP // SIZES[s]) + devices[0]
            ready = result.at[j, :, pl.ds(place * E, E)]

            @pl.when(j != me)
            def _():
                out_copy(j, ready, out_place(place, me)).start()

            @pl.when(j == me)
            def _():
                pltpu.make_async_copy(ready, out_place(place, me), out_keep).start()

    loaded(1, EVEN, (0, 1))
    outers(0)
    pl.semaphore_wait(barrier, CHIPS - 1 + NX + z)
    send_near(0)

    @pl.loop(0, z)
    def _(i):
        pl.semaphore_signal(z_ready, inc=1, device_id=depth(i), device_id_type=MESH)

    loaded(4, ODD, (2, 3))
    outers(1)
    send_near(1)
    loaded(3, EVEN, (4, 5))
    outers(2)
    send_near(2)
    forward(0)
    outers(3)
    send_near(3)
    forward(1)
    outers(4)
    send_near(4)
    forward(2)
    forward(3)
    forward(4)
    q_load.wait()
    inside_part(0, 8)
    gather_plane(0)
    share_gain()
    inside_part(8, 16)
    gather_plane(1)
    inside_part(16, 24)
    gather_plane(2)
    give_back(0)
    for s in range(len(SETS)):
        own_copy(s, c, rest_recv).start()
    inside_part(24, 32)
    gather_plane(3)
    give_back(1)
    gather_plane(4)
    give_back(2)
    give_back(3)
    give_back(4)
    gain_copy(0, gall.at[peers], gall.at[peers]).wait_recv()
    share(0)
    finish(0)
    share(1)
    finish(1)
    share(2)
    finish(2)
    share(3)
    finish(3)
    share(4)
    finish(4)

    arrived = out_hbm.at[pl.ds(0, (GROUP - 1) * TOKENS)]
    out_copy(me, arrived, arrived).wait_recv()
    kept = out_hbm.at[pl.ds(0, TOKENS)]
    pltpu.make_async_copy(kept, kept, out_keep).wait()
    out_copy(me, result.at[peers], result.at[peers]).wait_send()
    pltpu.make_async_remote_copy(own, own, own_send, rest_recv, device_id=other, device_id_type=MESH).wait_send()
    fwd_copy(0, n, coded.at[most], coded.at[most]).wait_send()
    back_copy(0, n, pcode.at[most], pcode.at[most]).wait_send()
    for count in range(1, NZ):
        @pl.when(z == NZ - 1 - count)
        def _():
            z_copy(0, z, zland.at[pl.ds(0, count)], zland.at[pl.ds(0, count)]).wait_send()
    pltpu.make_async_remote_copy(
        pstate.at[0], pstate.at[0], pair_send, pair_recv.at[0], device_id=other, device_id_type=MESH
    ).wait_send()
    gain_copy(0, gall.at[peers], gall.at[peers]).wait_send()


def shards(query_rows, key_rows, value_rows, norm_gain):
    tokens, width = query_rows.shape
    dma, per_set = pltpu.SemaphoreType.DMA, pltpu.SemaphoreType.DMA((len(SETS),))
    f32, bf16 = jnp.float32, jnp.bfloat16
    held = [
        pltpu.with_memory_space_constraint(rows, pltpu.HBM)
        for rows in (query_rows, key_rows, value_rows, norm_gain.reshape(1, PER_DEVICE * E))
    ]
    return pl.pallas_call(
        kernel,
        out_shape=jax.ShapeDtypeStruct((tokens * GROUP, width // GROUP), bf16),
        in_specs=[pl.BlockSpec(memory_space=pl.ANY)] * 4,
        out_specs=pl.BlockSpec(memory_space=pl.ANY),
        scratch_shapes=[
            pltpu.VMEM((tokens, width), bf16),
            pltpu.VMEM((tokens, width), bf16),
            pltpu.VMEM((tokens, width), bf16),
            pltpu.VMEM((CORES, CHIPS, E, E), f32),
            pltpu.VMEM((CORES, CHIPS, E, E), f32),
            pltpu.VMEM((HEADS, tokens, E), f32),
            pltpu.VMEM((CHIPS, E, E), bf16),
            pltpu.VMEM((CHIPS, E, E), bf16),
            pltpu.VMEM((CHIPS, E, E), f32),
            pltpu.VMEM((E, E), bf16),
            pltpu.VMEM((NZ, E, E), bf16),
            pltpu.VMEM((CHIPS, E, E), bf16),
            pltpu.VMEM((CORES, CHIPS, E, E), bf16),
            pltpu.VMEM((GROUP, tokens, PER_DEVICE * E), bf16),
            pltpu.VMEM((1, PER_DEVICE * E), f32),
            pltpu.VMEM((8, PER_DEVICE * E), f32),
            pltpu.VMEM((GROUP, 8, PER_DEVICE * E), f32),
            dma((8,)), dma, per_set, dma, dma, per_set, dma, per_set, dma, per_set, dma, per_set,
            dma, dma, dma, dma, dma,
            pltpu.SemaphoreType.REGULAR,
        ],
        compiler_params=pltpu.CompilerParams(
            collective_id=0, has_side_effects=True, vmem_limit_bytes=48 * 1024 * 1024
        ),
    )(*held)


def solution(mesh):
    placed = (
        P(("seq", "head"), None),
        P(("seq", "head"), None),
        P(("seq", "head"), None),
        P("head"),
    )
    return jax.shard_map(
        shards, mesh=mesh, in_specs=placed, out_specs=P("seq", "head"), check_vma=False
    )
```

```python
import jax
import jax.numpy as jnp
from jax import lax
from jax.experimental import pallas as pl
from jax.experimental.pallas import tpu as pltpu
from jax.sharding import PartitionSpec as P

E = 128
TOKENS = 256
HEADS = 32
NX, NY, NZ, CORES = 4, 4, 8, 2
CHIPS = NX * NY
GROUP = NX * CORES
PER_DEVICE = HEADS // GROUP
EVEN, ODD, EVERY = tuple(range(0, GROUP, 2)), tuple(range(1, GROUP, 2)), tuple(range(GROUP))
SETS = ((0, EVEN), (0, ODD), (1, EVERY), (2, EVERY), (3, EVERY))
SIZES = [len(devices) for _, devices in SETS]
SUBS = [CHIPS // size for size in SIZES]
PIECES = [E * size // HEADS for size in SIZES]
ROWS = [slice(sum(PIECES[:s]), sum(PIECES[:s + 1])) for s in range(len(SETS))]
SCALE = 1024.0
MESH = pl.DeviceIdType.MESH


def encode(state):
    scaled = state * SCALE
    return ((scaled * jnp.abs(scaled)) * (scaled * scaled)).astype(jnp.bfloat16)


def decode(code):
    wide = code.astype(jnp.float32)
    root = lax.rsqrt(lax.rsqrt(jnp.abs(wide))) * (1.0 / SCALE)
    return jnp.where(wide < 0.0, -root, root)


def kernel(q_hbm, k_hbm, v_hbm, gain_hbm, out_hbm,
           q, k, v, own, sib, within, coded, landed, ahead, zcode, zland, pcode, pstate, result, grow, gmine, gall,
           load_sem, own_send, near_recv, rest_recv, fwd_send, fwd_recv, z_send, z_recv, back_send, back_recv,
           pair_send, pair_recv, out_send, out_recv, out_keep, gain_send, gain_recv, z_ready):
    seq, me = lax.axis_index("seq"), lax.axis_index("head")
    z, y = lax.div(seq, NY), lax.rem(seq, NY)
    x, c = lax.div(me, CORES), lax.rem(me, CORES)
    n = y * NX + x
    other = (seq, x * CORES + 1 - c)

    def chip(a):
        return (z * NY + lax.div(a, NX), lax.rem(a, NX) * CORES + c)

    def depth(other_z):
        return (other_z * NY + y, me)

    def turned(i):
        return lax.rem(n + 1 + i, CHIPS)

    def columns(h):
        if isinstance(h, int):
            return pl.ds(h * E, E)
        return pl.ds(pl.multiple_of(h * E, E), E)

    def loads(first, width, devices, sems):
        for j in devices:
            part = pl.ds(j * PER_DEVICE * E + first * E, width * E)
            for source, target, sem in ((k_hbm, k, sems[0]), (v_hbm, v, sems[1])):
                pltpu.make_async_copy(source.at[:, part], target.at[:, part], load_sem.at[sem]).start()

    def loaded(width, devices, sems):
        part = pl.ds(0, width * len(devices) * E)
        for source, target, sem in ((k_hbm, k, sems[0]), (v_hbm, v, sems[1])):
            pltpu.make_async_copy(source.at[:, part], target.at[:, part], load_sem.at[sem]).wait()

    q_load = pltpu.make_async_copy(q_hbm, q, load_sem.at[6])
    gain_load = pltpu.make_async_copy(gain_hbm, grow, load_sem.at[7])
    barrier = pltpu.get_barrier_semaphore()

    @pl.loop(1, CHIPS)
    def _(i):
        pl.semaphore_signal(barrier, inc=1, device_id=chip(lax.rem(n + i, CHIPS)), device_id_type=MESH)

    @pl.loop(0, NX)
    def _(i):
        pl.semaphore_signal(
            barrier, inc=1, device_id=(seq, lax.rem(x + i, NX) * CORES + 1 - c), device_id_type=MESH
        )

    loads(0, 1, EVEN, (0, 1))
    loads(0, 4, ODD, (2, 3))
    loads(1, 3, EVEN, (4, 5))
    @pl.loop(z + 1, NZ)
    def _(i):
        pl.semaphore_signal(barrier, inc=1, device_id=depth(i), device_id_type=MESH)

    zland[...] = jnp.zeros_like(zland)

    q_load.start()
    gain_load.start()

    def outer(s, a):
        place, devices = SETS[s]
        col = columns(devices[a] * PER_DEVICE + place)
        state = lax.dot_general(k[:, col], v[:, col], (((0,), (0,)), ((), ())), preferred_element_type=jnp.float32)
        for sub in range(SUBS[s]):
            for core in range(CORES):
                row = (sub * CORES + core) * PIECES[s]
                own[core, a * SUBS[s] + sub, ROWS[s]] = state[row:row + PIECES[s]]

    def own_copy(s, core, sem):
        part = (core, slice(None), ROWS[s])
        return pltpu.make_async_remote_copy(
            own.at[part], sib.at[part], own_send, sem, device_id=other, device_id_type=MESH
        )

    def gain_copy(i, src, dst):
        return pltpu.make_async_remote_copy(
            src, dst, gain_send, gain_recv, device_id=(seq, lax.rem(me + i, GROUP)), device_id_type=MESH
        )

    def fwd_copy(s, a, src, dst):
        return pltpu.make_async_remote_copy(
            src, dst, fwd_send, fwd_recv.at[s], device_id=chip(a), device_id_type=MESH
        )

    def z_copy(s, i, src, dst):
        return pltpu.make_async_remote_copy(
            src, dst, z_send, z_recv.at[s], device_id=depth(i), device_id_type=MESH
        )

    def back_copy(s, a, src, dst):
        return pltpu.make_async_remote_copy(
            src, dst, back_send, back_recv.at[s], device_id=chip(a), device_id_type=MESH
        )

    def pair_copy(s, which):
        part = (which, slice(None), ROWS[s])
        return pltpu.make_async_remote_copy(
            pstate.at[part], pstate.at[part], pair_send, pair_recv.at[s], device_id=other, device_id_type=MESH
        )

    def out_place(place, j):
        return out_hbm.at[pl.ds(pl.multiple_of(j * TOKENS, TOKENS), TOKENS), pl.ds(place * E, E)]

    def out_copy(j, src, dst):
        return pltpu.make_async_remote_copy(src, dst, out_send, out_recv, device_id=(seq, j), device_id_type=MESH)

    most, peers = pl.ds(0, CHIPS - 1), pl.ds(0, GROUP - 1)

    def outers(s):
        for a in range(SIZES[s]):
            outer(s, a)

    def send_near(s):
        own_copy(s, 1 - c, near_recv.at[s]).start()

    def forward(s):
        own_copy(s, c, near_recv.at[s]).wait_recv()
        rows = ROWS[s]
        for i in range(CHIPS):
            a = turned(i)
            coded[i, rows] = encode(own[c, a, rows] + sib[c, a, rows])

        @pl.loop(0, CHIPS - 1)
        def _(i):
            fwd_copy(s, turned(i), coded.at[i, rows], landed.at[n, rows]).start()

        landed[n, rows] = coded[CHIPS - 1, rows]

    def share_gain():
        gain_load.wait()
        gmine[...] = jnp.broadcast_to(grow[...], gmine.shape)
        gall[me] = jnp.broadcast_to(grow[...], gmine.shape)

        @pl.loop(1, GROUP)
        def _(i):
            gain_copy(i, gmine, gall.at[me]).start()

    def inside_part(first, last):
        causal = lax.broadcasted_iota(jnp.int32, (TOKENS, TOKENS), 1) <= lax.broadcasted_iota(
            jnp.int32, (TOKENS, TOKENS), 0
        )

        @pl.loop(first // 8, last // 8)
        def _(group):
            for u in range(8):
                h = group * 8 + u
                col = columns(h)
                scores = lax.dot_general(
                    q[:, col], k[:, col], (((1,), (1,)), ((), ())), preferred_element_type=jnp.float32
                )
                weights = jnp.where(causal, scores, 0.0).astype(jnp.bfloat16)
                within[h] = jnp.dot(weights, v[:, col], preferred_element_type=jnp.float32)

    def gather_plane(s):
        rows = ROWS[s]
        fwd_copy(s, n, coded.at[most, rows], landed.at[most, rows]).wait_recv()
        total = jnp.zeros((PIECES[s], E), jnp.float32)
        for a in range(CHIPS):
            ahead[a, rows] = total
            total = total + decode(landed[a, rows])
        zcode[rows] = encode(total)
        if s == 0:
            @pl.when(z < NZ - 1)
            def _():
                pl.semaphore_wait(z_ready, NZ - 1 - z)

        @pl.loop(z + 1, NZ)
        def _(i):
            z_copy(s, i, zcode.at[rows], zland.at[z, rows]).start()

    def give_back(s):
        rows = ROWS[s]
        for count in range(1, NZ):
            @pl.when(z == count)
            def _():
                earlier = zland.at[pl.ds(0, count), rows]
                z_copy(s, z, earlier, earlier).wait_recv()

        base = decode(zland[0, rows])
        for i in range(1, NZ - 1):
            base = base + decode(zland[i, rows])
        for i in range(CHIPS):
            pcode[i, rows] = encode(base + ahead[turned(i), rows])

        @pl.loop(0, CHIPS - 1)
        def _(i):
            back_copy(s, turned(i), pcode.at[i, rows], pstate.at[c, n, rows]).start()

        pstate[c, n, rows] = pcode[CHIPS - 1, rows]

    def share(s):
        rows = ROWS[s]
        back_copy(s, n, pcode.at[most, rows], pstate.at[c, most, rows]).wait_recv()
        pair_copy(s, c).start()

    def finish(s):
        pair_copy(s, 1 - c).wait_recv()
        rows = ROWS[s]
        place, devices = SETS[s]
        if s == 0:
            everything = sib.at[1 - c]
            pltpu.make_async_remote_copy(
                everything, everything, own_send, rest_recv, device_id=other, device_id_type=MESH
            ).wait_recv()
        for t in range(SIZES[s]):
            a = lax.rem(x * SIZES[s] // NX + 1 + t, SIZES[s])
            j = a * (GROUP // SIZES[s]) + devices[0]
            h = j * PER_DEVICE + place
            pieces = [(core, a * SUBS[s] + sub) for sub in range(SUBS[s]) for core in range(CORES)]
            before = jnp.concatenate([decode(pstate[core, p, rows]) for core, p in pieces], axis=0)
            beside = jnp.concatenate([sib[core, p, rows] for core, p in pieces], axis=0)
            before = before + jnp.where(c == 1, beside, 0.0)
            high = before.astype(jnp.bfloat16)
            low = (before - high.astype(jnp.float32)).astype(jnp.bfloat16)
            queries = q[:, columns(h)]
            attended = (
                within[h]
                + jnp.dot(queries, high, preferred_element_type=jnp.float32)
                + jnp.dot(queries, low, preferred_element_type=jnp.float32)
            )
            mean = jnp.mean(attended * attended, axis=-1, keepdims=True)
            gain = gall[j, 0:1, place * E:(place + 1) * E]
            normed = attended * lax.rsqrt(mean + 1e-06) * gain
            result[j, :, place * E:(place + 1) * E] = normed.astype(jnp.bfloat16)

        @pl.loop(0, SIZES[s])
        def _(t):
            a = lax.rem(x * SIZES[s] // NX + 1 + t, SIZES[s])
            j = a * (GROUP // SIZES[s]) + devices[0]
            ready = result.at[j, :, pl.ds(place * E, E)]

            @pl.when(j != me)
            def _():
                out_copy(j, ready, out_place(place, me)).start()

            @pl.when(j == me)
            def _():
                pltpu.make_async_copy(ready, out_place(place, me), out_keep).start()

    loaded(1, EVEN, (0, 1))
    outers(0)
    pl.semaphore_wait(barrier, CHIPS - 1 + NX + z)
    send_near(0)

    @pl.loop(0, z)
    def _(i):
        pl.semaphore_signal(z_ready, inc=1, device_id=depth(i), device_id_type=MESH)

    loaded(4, ODD, (2, 3))
    outers(1)
    send_near(1)
    loaded(3, EVEN, (4, 5))
    outers(2)
    send_near(2)
    forward(0)
    outers(3)
    send_near(3)
    forward(1)
    outers(4)
    send_near(4)
    forward(2)
    forward(3)
    forward(4)
    q_load.wait()
    inside_part(0, 8)
    gather_plane(0)
    share_gain()
    inside_part(8, 16)
    gather_plane(1)
    inside_part(16, 24)
    gather_plane(2)
    give_back(0)
    for s in range(len(SETS)):
        own_copy(s, c, rest_recv).start()
    inside_part(24, 32)
    give_back(1)
    gather_plane(3)
    give_back(2)
    gather_plane(4)
    give_back(3)
    give_back(4)
    gain_copy(0, gall.at[peers], gall.at[peers]).wait_recv()
    share(0)
    finish(0)
    share(1)
    finish(1)
    share(2)
    finish(2)
    share(3)
    finish(3)
    share(4)
    finish(4)

    arrived = out_hbm.at[pl.ds(0, (GROUP - 1) * TOKENS)]
    out_copy(me, arrived, arrived).wait_recv()
    kept = out_hbm.at[pl.ds(0, TOKENS)]
    pltpu.make_async_copy(kept, kept, out_keep).wait()
    out_copy(me, result.at[peers], result.at[peers]).wait_send()
    pltpu.make_async_remote_copy(own, own, own_send, rest_recv, device_id=other, device_id_type=MESH).wait_send()
    fwd_copy(0, n, coded.at[most], coded.at[most]).wait_send()
    back_copy(0, n, pcode.at[most], pcode.at[most]).wait_send()
    for count in range(1, NZ):
        @pl.when(z == NZ - 1 - count)
        def _():
            z_copy(0, z, zland.at[pl.ds(0, count)], zland.at[pl.ds(0, count)]).wait_send()
    pltpu.make_async_remote_copy(
        pstate.at[0], pstate.at[0], pair_send, pair_recv.at[0], device_id=other, device_id_type=MESH
    ).wait_send()
    gain_copy(0, gall.at[peers], gall.at[peers]).wait_send()


def shards(query_rows, key_rows, value_rows, norm_gain):
    tokens, width = query_rows.shape
    dma, per_set = pltpu.SemaphoreType.DMA, pltpu.SemaphoreType.DMA((len(SETS),))
    f32, bf16 = jnp.float32, jnp.bfloat16
    held = [
        pltpu.with_memory_space_constraint(rows, pltpu.HBM)
        for rows in (query_rows, key_rows, value_rows, norm_gain.reshape(1, PER_DEVICE * E))
    ]
    return pl.pallas_call(
        kernel,
        out_shape=jax.ShapeDtypeStruct((tokens * GROUP, width // GROUP), bf16),
        in_specs=[pl.BlockSpec(memory_space=pl.ANY)] * 4,
        out_specs=pl.BlockSpec(memory_space=pl.ANY),
        scratch_shapes=[
            pltpu.VMEM((tokens, width), bf16),
            pltpu.VMEM((tokens, width), bf16),
            pltpu.VMEM((tokens, width), bf16),
            pltpu.VMEM((CORES, CHIPS, E, E), f32),
            pltpu.VMEM((CORES, CHIPS, E, E), f32),
            pltpu.VMEM((HEADS, tokens, E), f32),
            pltpu.VMEM((CHIPS, E, E), bf16),
            pltpu.VMEM((CHIPS, E, E), bf16),
            pltpu.VMEM((CHIPS, E, E), f32),
            pltpu.VMEM((E, E), bf16),
            pltpu.VMEM((NZ, E, E), bf16),
            pltpu.VMEM((CHIPS, E, E), bf16),
            pltpu.VMEM((CORES, CHIPS, E, E), bf16),
            pltpu.VMEM((GROUP, tokens, PER_DEVICE * E), bf16),
            pltpu.VMEM((1, PER_DEVICE * E), f32),
            pltpu.VMEM((8, PER_DEVICE * E), f32),
            pltpu.VMEM((GROUP, 8, PER_DEVICE * E), f32),
            dma((8,)), dma, per_set, dma, dma, per_set, dma, per_set, dma, per_set, dma, per_set,
            dma, dma, dma, dma, dma,
            pltpu.SemaphoreType.REGULAR,
        ],
        compiler_params=pltpu.CompilerParams(
            collective_id=0, has_side_effects=True, vmem_limit_bytes=48 * 1024 * 1024
        ),
    )(*held)


def solution(mesh):
    placed = (
        P(("seq", "head"), None),
        P(("seq", "head"), None),
        P(("seq", "head"), None),
        P("head"),
    )
    return jax.shard_map(
        shards, mesh=mesh, in_specs=placed, out_specs=P("seq", "head"), check_vma=False
    )
```

```python
import jax
import jax.numpy as jnp
from jax import lax
from jax.experimental import pallas as pl
from jax.experimental.pallas import tpu as pltpu
from jax.sharding import PartitionSpec as P

E = 128
TOKENS = 256
HEADS = 32
NX, NY, NZ, CORES = 4, 4, 8, 2
CHIPS = NX * NY
GROUP = NX * CORES
PER_DEVICE = HEADS // GROUP
EVEN, ODD, EVERY = tuple(range(0, GROUP, 2)), tuple(range(1, GROUP, 2)), tuple(range(GROUP))
SETS = ((0, EVEN), (0, ODD), (1, EVERY), (2, EVERY), (3, EVERY))
SIZES = [len(devices) for _, devices in SETS]
SUBS = [CHIPS // size for size in SIZES]
PIECES = [E * size // HEADS for size in SIZES]
ROWS = [slice(sum(PIECES[:s]), sum(PIECES[:s + 1])) for s in range(len(SETS))]
SCALE = 1024.0
MESH = pl.DeviceIdType.MESH


def encode(state):
    scaled = state * SCALE
    return ((scaled * jnp.abs(scaled)) * (scaled * scaled)).astype(jnp.bfloat16)


def decode(code):
    wide = code.astype(jnp.float32)
    root = lax.rsqrt(lax.rsqrt(jnp.abs(wide))) * (1.0 / SCALE)
    return jnp.where(wide < 0.0, -root, root)


def kernel(q_hbm, k_hbm, v_hbm, gain_hbm, out_hbm,
           q, k, v, own, sib, within, coded, landed, ahead, zcode, zland, pcode, pstate, result, grow, gmine, gall,
           load_sem, own_send, near_recv, rest_recv, fwd_send, fwd_recv, z_send, z_recv, back_send, back_recv,
           pair_send, pair_recv, out_send, out_recv, out_keep, gain_send, gain_recv, z_ready):
    seq, me = lax.axis_index("seq"), lax.axis_index("head")
    z, y = lax.div(seq, NY), lax.rem(seq, NY)
    x, c = lax.div(me, CORES), lax.rem(me, CORES)
    n = y * NX + x
    other = (seq, x * CORES + 1 - c)

    def chip(a):
        return (z * NY + lax.div(a, NX), lax.rem(a, NX) * CORES + c)

    def depth(other_z):
        return (other_z * NY + y, me)

    def turned(i):
        return lax.rem(n + 1 + i + c * (CHIPS - 2 - 2 * i), CHIPS)

    def columns(h):
        if isinstance(h, int):
            return pl.ds(h * E, E)
        return pl.ds(pl.multiple_of(h * E, E), E)

    def loads(first, width, devices, sems):
        for j in devices:
            part = pl.ds(j * PER_DEVICE * E + first * E, width * E)
            for source, target, sem in ((k_hbm, k, sems[0]), (v_hbm, v, sems[1])):
                pltpu.make_async_copy(source.at[:, part], target.at[:, part], load_sem.at[sem]).start()

    def loaded(width, devices, sems):
        part = pl.ds(0, width * len(devices) * E)
        for source, target, sem in ((k_hbm, k, sems[0]), (v_hbm, v, sems[1])):
            pltpu.make_async_copy(source.at[:, part], target.at[:, part], load_sem.at[sem]).wait()

    q_load = pltpu.make_async_copy(q_hbm, q, load_sem.at[6])
    gain_load = pltpu.make_async_copy(gain_hbm, grow, load_sem.at[7])
    barrier = pltpu.get_barrier_semaphore()

    @pl.loop(1, CHIPS)
    def _(i):
        pl.semaphore_signal(barrier, inc=1, device_id=chip(lax.rem(n + i, CHIPS)), device_id_type=MESH)

    @pl.loop(0, NX)
    def _(i):
        pl.semaphore_signal(
            barrier, inc=1, device_id=(seq, lax.rem(x + i, NX) * CORES + 1 - c), device_id_type=MESH
        )

    loads(0, 1, EVEN, (0, 1))
    loads(0, 4, ODD, (2, 3))
    loads(1, 3, EVEN, (4, 5))
    @pl.loop(z + 1, NZ)
    def _(i):
        pl.semaphore_signal(barrier, inc=1, device_id=depth(i), device_id_type=MESH)

    zland[...] = jnp.zeros_like(zland)

    q_load.start()
    gain_load.start()

    def outer(s, a):
        place, devices = SETS[s]
        col = columns(devices[a] * PER_DEVICE + place)
        state = lax.dot_general(k[:, col], v[:, col], (((0,), (0,)), ((), ())), preferred_element_type=jnp.float32)
        for sub in range(SUBS[s]):
            for core in range(CORES):
                row = (sub * CORES + core) * PIECES[s]
                own[core, a * SUBS[s] + sub, ROWS[s]] = state[row:row + PIECES[s]]

    def own_copy(s, core, sem):
        part = (core, slice(None), ROWS[s])
        return pltpu.make_async_remote_copy(
            own.at[part], sib.at[part], own_send, sem, device_id=other, device_id_type=MESH
        )

    def gain_copy(i, src, dst):
        return pltpu.make_async_remote_copy(
            src, dst, gain_send, gain_recv, device_id=(seq, lax.rem(me + i, GROUP)), device_id_type=MESH
        )

    def fwd_copy(s, a, src, dst):
        return pltpu.make_async_remote_copy(
            src, dst, fwd_send, fwd_recv.at[s], device_id=chip(a), device_id_type=MESH
        )

    def z_copy(s, i, src, dst):
        return pltpu.make_async_remote_copy(
            src, dst, z_send, z_recv.at[s], device_id=depth(i), device_id_type=MESH
        )

    def back_copy(s, a, src, dst):
        return pltpu.make_async_remote_copy(
            src, dst, back_send, back_recv.at[s], device_id=chip(a), device_id_type=MESH
        )

    def pair_copy(s, which):
        part = (which, slice(None), ROWS[s])
        return pltpu.make_async_remote_copy(
            pstate.at[part], pstate.at[part], pair_send, pair_recv.at[s], device_id=other, device_id_type=MESH
        )

    def out_place(place, j):
        return out_hbm.at[pl.ds(pl.multiple_of(j * TOKENS, TOKENS), TOKENS), pl.ds(place * E, E)]

    def out_copy(j, src, dst):
        return pltpu.make_async_remote_copy(src, dst, out_send, out_recv, device_id=(seq, j), device_id_type=MESH)

    most, peers = pl.ds(0, CHIPS - 1), pl.ds(0, GROUP - 1)

    def outers(s):
        for a in range(SIZES[s]):
            outer(s, a)

    def send_near(s):
        own_copy(s, 1 - c, near_recv.at[s]).start()

    def forward(s):
        own_copy(s, c, near_recv.at[s]).wait_recv()
        rows = ROWS[s]
        for i in range(CHIPS):
            a = turned(i)
            coded[i, rows] = encode(own[c, a, rows] + sib[c, a, rows])

        @pl.loop(0, CHIPS - 1)
        def _(i):
            fwd_copy(s, turned(i), coded.at[i, rows], landed.at[n, rows]).start()

        landed[n, rows] = coded[CHIPS - 1, rows]

    def share_gain():
        gain_load.wait()
        gmine[...] = jnp.broadcast_to(grow[...], gmine.shape)
        gall[me] = jnp.broadcast_to(grow[...], gmine.shape)

        @pl.loop(1, GROUP)
        def _(i):
            gain_copy(i, gmine, gall.at[me]).start()

    def inside_part(first, last):
        causal = lax.broadcasted_iota(jnp.int32, (TOKENS, TOKENS), 1) <= lax.broadcasted_iota(
            jnp.int32, (TOKENS, TOKENS), 0
        )

        @pl.loop(first // 8, last // 8)
        def _(group):
            for u in range(8):
                h = group * 8 + u
                col = columns(h)
                scores = lax.dot_general(
                    q[:, col], k[:, col], (((1,), (1,)), ((), ())), preferred_element_type=jnp.float32
                )
                weights = jnp.where(causal, scores, 0.0).astype(jnp.bfloat16)
                within[h] = jnp.dot(weights, v[:, col], preferred_element_type=jnp.float32)

    def gather_plane(s):
        rows = ROWS[s]
        fwd_copy(s, n, coded.at[most, rows], landed.at[most, rows]).wait_recv()
        total = jnp.zeros((PIECES[s], E), jnp.float32)
        for a in range(CHIPS):
            ahead[a, rows] = total
            total = total + decode(landed[a, rows])
        zcode[rows] = encode(total)
        if s == 0:
            @pl.when(z < NZ - 1)
            def _():
                pl.semaphore_wait(z_ready, NZ - 1 - z)

        @pl.loop(z + 1, NZ)
        def _(i):
            z_copy(s, i, zcode.at[rows], zland.at[z, rows]).start()

    def give_back(s):
        rows = ROWS[s]
        for count in range(1, NZ):
            @pl.when(z == count)
            def _():
                earlier = zland.at[pl.ds(0, count), rows]
                z_copy(s, z, earlier, earlier).wait_recv()

        base = decode(zland[0, rows])
        for i in range(1, NZ - 1):
            base = base + decode(zland[i, rows])
        for i in range(CHIPS):
            pcode[i, rows] = encode(base + ahead[turned(i), rows])

        @pl.loop(0, CHIPS - 1)
        def _(i):
            back_copy(s, turned(i), pcode.at[i, rows], pstate.at[c, n, rows]).start()

        pstate[c, n, rows] = pcode[CHIPS - 1, rows]

    def share(s):
        rows = ROWS[s]
        back_copy(s, n, pcode.at[most, rows], pstate.at[c, most, rows]).wait_recv()
        pair_copy(s, c).start()

    def target(s, t):
        per_chip = SIZES[s] // NX
        step = (1, 3, 1, 3, 2, 2, 0, 0)[t] if per_chip == 2 else (1, 3, 2, 0)[t]
        bit = (0, 0, 1, 1, 0, 1, 0, 1)[t] if per_chip == 2 else 0
        dest = lax.rem(x + step + c * ((NX - 2 * step) if step % 2 else 0), NX)
        a = dest * per_chip + bit
        return a, a * (GROUP // SIZES[s]) + SETS[s][1][0]

    def keep_or_send(j, ready, place):
        @pl.when(j != me)
        def _():
            out_copy(j, ready, out_place(place, me)).start()

        @pl.when(j == me)
        def _():
            pltpu.make_async_copy(ready, out_place(place, me), out_keep).start()

    def finish(s):
        pair_copy(s, 1 - c).wait_recv()
        rows = ROWS[s]
        place, devices = SETS[s]
        if s == 0:
            everything = sib.at[1 - c]
            pltpu.make_async_remote_copy(
                everything, everything, own_send, rest_recv, device_id=other, device_id_type=MESH
            ).wait_recv()
        for t in range(SIZES[s]):
            a, j = target(s, t)
            h = j * PER_DEVICE + place
            pieces = [(core, a * SUBS[s] + sub) for sub in range(SUBS[s]) for core in range(CORES)]
            before = jnp.concatenate([decode(pstate[core, p, rows]) for core, p in pieces], axis=0)
            beside = jnp.concatenate([sib[core, p, rows] for core, p in pieces], axis=0)
            before = before + jnp.where(c == 1, beside, 0.0)
            high = before.astype(jnp.bfloat16)
            low = (before - high.astype(jnp.float32)).astype(jnp.bfloat16)
            queries = q[:, columns(h)]
            attended = (
                within[h]
                + jnp.dot(queries, high, preferred_element_type=jnp.float32)
                + jnp.dot(queries, low, preferred_element_type=jnp.float32)
            )
            mean = jnp.mean(attended * attended, axis=-1, keepdims=True)
            gain = gall[j, 0:1, place * E:(place + 1) * E]
            normed = attended * lax.rsqrt(mean + 1e-06) * gain
            result[j, :, place * E:(place + 1) * E] = normed.astype(jnp.bfloat16)

        for t in range(SIZES[s]):
            _, j = target(s, t)
            ready = result.at[j, :, pl.ds(place * E, E)]
            if t < SIZES[s] - SIZES[s] // NX:
                out_copy(j, ready, out_place(place, me)).start()
            else:
                keep_or_send(j, ready, place)

    loaded(1, EVEN, (0, 1))
    outers(0)
    pl.semaphore_wait(barrier, CHIPS - 1 + NX + z)
    send_near(0)

    @pl.loop(0, z)
    def _(i):
        pl.semaphore_signal(z_ready, inc=1, device_id=depth(i), device_id_type=MESH)

    loaded(4, ODD, (2, 3))
    outers(1)
    send_near(1)
    loaded(3, EVEN, (4, 5))
    outers(2)
    send_near(2)
    forward(0)
    outers(3)
    send_near(3)
    forward(1)
    outers(4)
    send_near(4)
    forward(2)
    forward(3)
    forward(4)
    q_load.wait()
    inside_part(0, 8)
    gather_plane(0)
    share_gain()
    inside_part(8, 16)
    gather_plane(1)
    inside_part(16, 24)
    gather_plane(2)
    give_back(0)
    for s in range(len(SETS)):
        own_copy(s, c, rest_recv).start()
    inside_part(24, 32)
    give_back(1)
    gather_plane(3)
    give_back(2)
    gather_plane(4)
    give_back(3)
    give_back(4)
    gain_copy(0, gall.at[peers], gall.at[peers]).wait_recv()
    share(0)
    finish(0)
    share(1)
    finish(1)
    share(2)
    finish(2)
    share(3)
    finish(3)
    share(4)
    finish(4)

    arrived = out_hbm.at[pl.ds(0, (GROUP - 1) * TOKENS)]
    out_copy(me, arrived, arrived).wait_recv()
    kept = out_hbm.at[pl.ds(0, TOKENS)]
    pltpu.make_async_copy(kept, kept, out_keep).wait()
    out_copy(me, result.at[peers], result.at[peers]).wait_send()
    pltpu.make_async_remote_copy(own, own, own_send, rest_recv, device_id=other, device_id_type=MESH).wait_send()
    fwd_copy(0, n, coded.at[most], coded.at[most]).wait_send()
    back_copy(0, n, pcode.at[most], pcode.at[most]).wait_send()
    for count in range(1, NZ):
        @pl.when(z == NZ - 1 - count)
        def _():
            z_copy(0, z, zland.at[pl.ds(0, count)], zland.at[pl.ds(0, count)]).wait_send()
    pltpu.make_async_remote_copy(
        pstate.at[0], pstate.at[0], pair_send, pair_recv.at[0], device_id=other, device_id_type=MESH
    ).wait_send()
    gain_copy(0, gall.at[peers], gall.at[peers]).wait_send()


def shards(query_rows, key_rows, value_rows, norm_gain):
    tokens, width = query_rows.shape
    dma, per_set = pltpu.SemaphoreType.DMA, pltpu.SemaphoreType.DMA((len(SETS),))
    f32, bf16 = jnp.float32, jnp.bfloat16
    held = [
        pltpu.with_memory_space_constraint(rows, pltpu.HBM)
        for rows in (query_rows, key_rows, value_rows, norm_gain.reshape(1, PER_DEVICE * E))
    ]
    return pl.pallas_call(
        kernel,
        out_shape=jax.ShapeDtypeStruct((tokens * GROUP, width // GROUP), bf16),
        in_specs=[pl.BlockSpec(memory_space=pl.ANY)] * 4,
        out_specs=pl.BlockSpec(memory_space=pl.ANY),
        scratch_shapes=[
            pltpu.VMEM((tokens, width), bf16),
            pltpu.VMEM((tokens, width), bf16),
            pltpu.VMEM((tokens, width), bf16),
            pltpu.VMEM((CORES, CHIPS, E, E), f32),
            pltpu.VMEM((CORES, CHIPS, E, E), f32),
            pltpu.VMEM((HEADS, tokens, E), f32),
            pltpu.VMEM((CHIPS, E, E), bf16),
            pltpu.VMEM((CHIPS, E, E), bf16),
            pltpu.VMEM((CHIPS, E, E), f32),
            pltpu.VMEM((E, E), bf16),
            pltpu.VMEM((NZ, E, E), bf16),
            pltpu.VMEM((CHIPS, E, E), bf16),
            pltpu.VMEM((CORES, CHIPS, E, E), bf16),
            pltpu.VMEM((GROUP, tokens, PER_DEVICE * E), bf16),
            pltpu.VMEM((1, PER_DEVICE * E), f32),
            pltpu.VMEM((8, PER_DEVICE * E), f32),
            pltpu.VMEM((GROUP, 8, PER_DEVICE * E), f32),
            dma((8,)), dma, per_set, dma, dma, per_set, dma, per_set, dma, per_set, dma, per_set,
            dma, dma, dma, dma, dma,
            pltpu.SemaphoreType.REGULAR,
        ],
        compiler_params=pltpu.CompilerParams(
            collective_id=0, has_side_effects=True, vmem_limit_bytes=48 * 1024 * 1024
        ),
    )(*held)


def solution(mesh):
    placed = (
        P(("seq", "head"), None),
        P(("seq", "head"), None),
        P(("seq", "head"), None),
        P("head"),
    )
    return jax.shard_map(
        shards, mesh=mesh, in_specs=placed, out_specs=P("seq", "head"), check_vma=False
    )
```
